1024 devices in a mesh: mem: 4 (over y_lo, core), lat: 8 (over x), lon: 32 (over z, y_hi).
Axes of the slice: x: 8, y: 8 (y_hi: 4, y_lo: 2; y = y_hi * 2 + y_lo), z: 8, core: 2. Of those that a mesh axis runs over, the one named last changes fastest.
Arguments:
- perturbations: bfloat16 [8, 4, 768, 1536], P('mem', None, 'lat', 'lon'), may hold values from -2 to 2
- innovation: float32 [8, 65536], P('lat', 'lon'), may hold values from -4.2 to 4.2
- obs_weight: float32 [8, 65536], P('lat', 'lon'), may hold values from 0.5 to 6, as said below
- obs_cell: int32 [8, 65536], P('lat', 'lon'), may hold values from 0 to 4607
- obs_level: int32 [8, 65536], P('lat', 'lon'), may hold values from 0 to 3
- cutoff: int32 [4], replicated, may hold values from 16 to 127
Outputs:
- solution: float32 [8, 4, 768, 512], P('mem', None, ('lat', 'lon'))
- residual: float32 [8, 4, 768, 512], P('mem', None, ('lat', 'lon'))
The draws below stay inside these ranges and needn't reach their ends.
Inputs may be any that keep to these rules, and one draw needn't show every extreme that they name: `obs_weight`: positive weights.
All inputs are finite; a program needn't handle non-finite values.
Results may differ from the reference program's by a relative error of at most 0.0008.
Values may be sent and summed in bfloat16 or wider, within the bound.
A program may use at most 32 MiB of HBM per device.

```python
import jax
import jax.numpy as jnp
from jax import lax

NLAT = 768
NLON = 1536
KMAX = 256
LEV = 4
ITERS = 2
OBS_DEV = 2048
MEMBERS = 8
TILE_LAT = 96
TILE_LON = 48
N_LAT = 8
N_LON = 32


def draw_obs_weight(key, part):
    array_shape = (N_LAT, N_LON * OBS_DEV)
    first_key = jax.random.fold_in(key, 11)
    row_index = jnp.arange(N_LAT, dtype=jnp.int32)[:, None]
    col_block = jnp.arange(N_LON * OBS_DEV, dtype=jnp.int32)[None, :] // OBS_DEV
    position = (row_index * N_LON + col_block).astype(jnp.float32) / (N_LAT * N_LON - 1)
    growth_factor = 1.0 + 2.0 * position
    spread_draw = jnp.exp(jax.random.uniform(first_key, array_shape, jnp.float32, jnp.log(0.5), jnp.log(2.0)))
    return (spread_draw * growth_factor).astype(jnp.float32)


def with_ends(drawn, own_key, smallest, largest):
    longest = drawn.shape.index(max(drawn.shape))
    spots = []
    for shift in (0, 1):
        where = [jax.random.randint(jax.random.fold_in(own_key, axis), (), 0, length) for axis, length in enumerate(drawn.shape)]
        where[longest] = (where[longest] + shift) % drawn.shape[longest]
        spots.append(tuple(where))
    return drawn.at[spots[0]].set(smallest).at[spots[1]].set(largest)


def block_levels(own_key, dims, pieces, low, largest):
    gain, own = 1.0, jax.random.fold_in(own_key, 6)
    for dim, parts in pieces:
        draws = jnp.exp(jax.random.uniform(jax.random.fold_in(own, dim), (parts,), jnp.float32, low / len(pieces), largest / len(pieces)))
        gain = gain * jnp.repeat(draws, dims[dim] // parts).reshape([-1 if axis == dim else 1 for axis in range(len(dims))])
    return gain


def normal_values(stream_key, extent, spread, reach, pieces=(), kind=jnp.bfloat16):
    result = spread * jax.random.normal(stream_key, extent, jnp.float32)
    if pieces:
        result = result * block_levels(stream_key, extent, pieces, -0.22, 0.18)
    return jnp.clip(result, -reach, reach).astype(kind)


def setup_inputs(seed: int = 0) -> dict:
    streams_of = jax.random.split(jax.random.key(seed), 7)
    perturbations = normal_values(streams_of[0], (MEMBERS, LEV, NLAT, NLON), MEMBERS ** -0.5, 2.0, ((0, 4), (2, 8), (3, 32)))
    innovation = normal_values(streams_of[1], (N_LAT, N_LON * OBS_DEV), 0.7, 4.2, ((0, 8), (1, 32)), jnp.float32)
    obs_weight = draw_obs_weight(jax.random.fold_in(streams_of[6], 71), 0)
    obs_cell = with_ends(jax.random.randint(streams_of[3], (N_LAT, N_LON * OBS_DEV), 0, TILE_LAT * TILE_LON), jax.random.fold_in(streams_of[3], 1), 0, (TILE_LAT * TILE_LON) - 1).astype(jnp.int32)
    obs_level = with_ends(jax.random.randint(streams_of[4], (N_LAT, N_LON * OBS_DEV), 0, LEV), jax.random.fold_in(streams_of[4], 1), 0, LEV - 1).astype(jnp.int32)
    cutoff = with_ends(jax.random.randint(streams_of[5], (LEV,), KMAX // 16, KMAX // 2), jax.random.fold_in(streams_of[5], 1), KMAX // 16, (KMAX // 2) - 1).astype(jnp.int32)
    return dict(perturbations=perturbations, innovation=innovation, obs_weight=obs_weight, obs_cell=obs_cell, obs_level=obs_level, cutoff=cutoff)


def basis_table():
    columns = jnp.arange(NLON, dtype=jnp.int32)[:, None]
    cos_waves = jnp.arange(KMAX, dtype=jnp.int32)[None, :]
    sin_waves = cos_waves + 1
    factor = 2.0 * jnp.pi / NLON
    cos_phase = (columns * cos_waves % NLON).astype(jnp.float32) * factor
    sin_phase = (columns * sin_waves % NLON).astype(jnp.float32) * factor
    joined = jnp.concatenate([jnp.cos(cos_phase), jnp.sin(sin_phase)], axis=1)
    return (joined / jnp.sqrt(jnp.float32(KMAX))).astype(jnp.float32)

def spectrum_of(cutoff):
    wavenumbers = jnp.concatenate([jnp.arange(KMAX, dtype=jnp.float32), jnp.arange(1, KMAX + 1, dtype=jnp.float32)])
    scaled = wavenumbers[None, :] / cutoff.astype(jnp.float32)[:, None]
    return 1.0 / (1.0 + scaled * scaled)

def reference(perturbations, innovation, obs_weight, obs_cell, obs_level, cutoff):
    basis = basis_table()
    spectrum = spectrum_of(cutoff)
    row_index = jnp.arange(N_LAT, dtype=jnp.int32)[:, None] * TILE_LAT + obs_cell // TILE_LON
    col_index = jnp.arange(N_LON * OBS_DEV, dtype=jnp.int32)[None, :] // OBS_DEV * TILE_LON + obs_cell % TILE_LON
    located = ((obs_level * NLAT + row_index) * NLON + col_index).reshape(-1).astype(jnp.int32)
    weights = obs_weight.reshape(-1)

    def gridded_of(weighted):
        field = jnp.zeros((LEV * NLAT * NLON,), jnp.float32).at[located].add(weighted)
        return field.reshape(LEV, NLAT, NLON)

    def synthesize(control):

        def one_member(carry, paired):
            member_pert, member_ctrl = paired
            coeffs = member_ctrl * spectrum[:, None, :]
            synthesized = jnp.dot(coeffs.reshape(-1, 2 * KMAX), basis.T, precision=lax.Precision.HIGHEST, preferred_element_type=jnp.float32)
            synthesized = synthesized.reshape(LEV, NLAT, NLON)
            return (carry + member_pert.astype(jnp.float32) * synthesized, None)
        total, unused = lax.scan(one_member, jnp.zeros((LEV, NLAT, NLON), jnp.float32), (perturbations, control))
        return total

    def analyse(gridded):

        def one_member(member_pert):
            products = member_pert.astype(jnp.float32) * gridded
            summed = jnp.dot(products.reshape(-1, NLON), basis, precision=lax.Precision.HIGHEST, preferred_element_type=jnp.float32)
            return summed.reshape(LEV, NLAT, 2 * KMAX) * spectrum[:, None, :]
        return lax.map(one_member, perturbations)

    def hessian(direction):
        increment = synthesize(direction)
        sampled = increment.reshape(-1)[located]
        return direction + analyse(gridded_of(weights * sampled))
    right_side = analyse(gridded_of(weights * innovation.reshape(-1)))
    solution = jnp.zeros_like(right_side)
    residual = right_side
    direction = right_side
    norm_now = jnp.sum(residual * residual)
    for iteration in range(ITERS):
        image = hessian(direction)
        step_size = norm_now / jnp.sum(direction * image)
        solution = solution + step_size * direction
        residual = residual - step_size * image
        norm_next = jnp.sum(residual * residual)
        direction = residual + norm_next / norm_now * direction
        norm_now = norm_next
    return (solution, residual)
```

```python
import jax
import jax.numpy as jnp
import ml_dtypes
import numpy as np
from jax import lax
from jax.experimental import pallas as pl
from jax.experimental.pallas import tpu as pltpu
from jax.sharding import PartitionSpec as P

MESH = pl.DeviceIdType.MESH
BF16 = jnp.bfloat16
F32 = jnp.float32
NLON = 1536
KMAX = 256
MEMBERS = 8
N_MEM = 4
N_LAT = 8
N_LON = 32
ROWS = 96
COLS = 48
LINES = 3
QUARTER = NLON // 4
SLOT = 16


def halves(table):
    high = table.astype(ml_dtypes.bfloat16)
    low = (table - high.astype(np.float64)).astype(ml_dtypes.bfloat16)
    return np.stack([high, low])


def constants():
    piece, source, i = np.meshgrid(np.arange(3), np.arange(8), np.arange(16), indexing="ij")
    column = (48 * source + 16 * piece + i).reshape(-1)

    def table(columns, cosines, sines):
        angle = 2.0 * np.pi / NLON
        cos = np.cos((columns[:, None] * cosines[None] % NLON) * angle)
        sin = np.sin((columns[:, None] * sines[None] % NLON) * angle)
        return np.concatenate([cos, sin], axis=1) / 16.0

    c0, s0 = np.arange(0, 256, 4), np.arange(4, 257, 4)
    c2 = np.arange(2, 256, 4)
    c1 = np.arange(1, 256, 2)
    t0 = table(column, c0, s0)
    t2 = table(column, c2, c2)
    t1 = table(np.concatenate([column, QUARTER + column]), c1, c1)
    wave = np.concatenate([c0, s0, c2, c2, c1, c1])
    natural = np.concatenate([c0, 255 + s0, c2, 255 + c2, c1, 255 + c1])
    order = np.zeros((512, 512))
    order[np.arange(512), natural] = 1

    pack = np.zeros((5, N_LON * SLOT, ROWS))
    unpack = np.zeros((216, 128))
    for s in range(LINES):
        for u in range(5):
            peer = np.arange(N_LON)
            pack[u, peer * SLOT + 3 * u + s, 3 * peer + s] = 1
        for piece in range(3):
            for m in range(MEMBERS):
                row = piece * 24 + s * 8 + m
                unpack[row, m * SLOT + piece * 3 + s] = 1
                for f in range(2):
                    for h in range(2):
                        r = (9, 12, 9)[piece] + s
                        q = (0, 0, 4)[piece] + 2 * f + h
                        unpack[72 * (f + 1) + row, q * SLOT + r] = 1
    small = [a.astype(ml_dtypes.bfloat16) for a in (pack, unpack)]
    tables = [halves(t) for t in (t0, t2, t1, t0.T, t2.T, t1.T)]
    return small + tables + [order.astype(ml_dtypes.bfloat16), np.broadcast_to(wave, (8, 512)).astype(np.float32)]


def dot(a, b):
    return jnp.dot(a, b, preferred_element_type=F32)


def dot_nt(a, b):
    return lax.dot_general(a, b, (((1,), (1,)), ((), ())), preferred_element_type=F32)


def split(x):
    high = x.astype(BF16)
    return high, (x - high.astype(F32)).astype(BF16)


def dot3(x, table):
    high, low = split(x)
    both = dot(jnp.concatenate([high, low], axis=0), table[0])
    n = x.shape[0]
    return both[:n] + (both[n:] + dot(high, table[1]))


def kernel(p_ref, inn_in, wt_in, cell_in, lev_in, cut_ref, *refs):
    n_const = 10
    loads_in = (inn_in, wt_in, cell_in, lev_in) + refs[:n_const]
    sol_ref, res_ref = refs[n_const : n_const + 2]
    scratch = refs[n_const + 2 :]
    n_load = n_const + 4
    loads_ref = scratch[:n_load]
    (mine, packed, got, x_ref, g_ref, n_ref, c_ref, out_c, in_c, part1, sums1, part2, sums2, last) = scratch[n_load : n_load + 14]
    load_sem, send_a, recv_a, send_b, recv_b, send_c, recv_c, send_s, recv_s = scratch[n_load + 14 :]
    inn_ref, wt_ref, cell_ref, lev_ref, pack, unpack, t0, t2, t1, b0, b2, b1, order, wave = loads_ref

    mem, lat, lon = lax.axis_index("mem"), lax.axis_index("lat"), lax.axis_index("lon")
    group = mem * N_LAT + lat

    def lon_peer(d):
        return {"mem": mem, "lat": lat, "lon": lax.rem(lon + d, N_LON)}

    def group_peer(d):
        other = lax.rem(group + d, N_MEM * N_LAT)
        return {"mem": other // N_LAT, "lat": lax.rem(other, N_LAT), "lon": lon}

    def mem_peer(d):
        return {"mem": lax.rem(mem + d, N_MEM), "lat": lat, "lon": lon}

    barrier = pltpu.get_barrier_semaphore()

    @pl.loop(1, 32)
    def _(d):
        pl.semaphore_signal(barrier, inc=1, device_id=group_peer(d), device_id_type=MESH)
        pl.semaphore_signal(barrier, inc=1, device_id=lon_peer(d), device_id_type=MESH)

    loads = [pltpu.make_async_copy(loads_in[k], loads_ref[k], load_sem.at[k]) for k in range(n_load)]
    for copy in loads:
        copy.start()
    own_members = pltpu.make_async_copy(p_ref.at[:, mem], mine.at[mem], load_sem.at[n_load])
    own_members.start()

    out_c[...] = jnp.zeros_like(out_c)

    for k in range(4):
        loads[k].wait()
    cell = cell_ref[...].astype(F32)
    row_of = jnp.floor((cell + 0.5) * (1.0 / COLS))
    col_of = cell - COLS * row_of
    key = row_of + ROWS * lev_ref[...].astype(F32)
    rows = lax.broadcasted_iota(jnp.int32, (ROWS, 1), 0) + ROWS * mem
    row_hot = jnp.where(rows.astype(F32) == key, 1.0, 0.0).astype(BF16)
    weight = wt_ref[...]
    col_hit = lax.broadcasted_iota(jnp.int32, (COLS, 1), 0).astype(F32) == col_of
    tile = jnp.zeros((2 * COLS, ROWS), F32)
    parts = [split(weight * inn_ref[...]), split(weight)]
    for h in range(2):
        placed = jnp.concatenate([jnp.where(col_hit, part[h].astype(F32), 0.0) for part in parts], axis=0).astype(BF16)
        tile += dot_nt(placed, row_hot)
    tiles = split(tile)

    def of_fields(piece):
        return [tiles[h][f * COLS + piece * 16 : f * COLS + piece * 16 + 16] for f in range(2) for h in range(2)]

    nothing = jnp.zeros((64, ROWS), BF16)
    chunks = [jnp.concatenate(of_fields(0) + of_fields(2), axis=0), jnp.concatenate(of_fields(1) + [nothing], axis=0)]
    loads[4].wait()
    message = dot_nt(pack[3], chunks[0]) + dot_nt(pack[4], chunks[1])

    pl.semaphore_wait(barrier, 62)

    for d in (2, 3, 1):
        peer = mem_peer(d)
        pltpu.make_async_remote_copy(
            p_ref.at[:, peer["mem"]], mine.at[mem], send_a, recv_a, device_id=peer, device_id_type=MESH
        ).start()
    own_members.wait()
    three = mine.at[pl.ds(0, 3)]
    pltpu.make_async_copy(three, three, recv_a).wait()
    for piece in range(3):
        chunk = [mine[k, a, piece * 16 : piece * 16 + 16, :] for k in range(N_MEM) for a in range(2)]
        message += dot_nt(pack[piece], jnp.concatenate(chunk, axis=0))
    packed[...] = message.astype(BF16).reshape(N_LON, SLOT, 128)

    @pl.loop(1, 32)
    def _(d):
        peer = lon_peer(d)
        pltpu.make_async_remote_copy(
            packed.at[peer["lon"]], got.at[lon], send_b, recv_b, device_id=peer, device_id_type=MESH
        ).start()

    got[lon] = packed[lon]
    for copy in loads[5:]:
        copy.wait()
    cutoff = cut_ref[mem].astype(F32)
    scaled = wave[0:1, :] / cutoff
    spectrum = 1.0 / (1.0 + scaled * scaled)
    lots = got.at[pl.ds(0, 31)]
    pltpu.make_async_copy(lots, lots, recv_b).wait()

    lane = lax.broadcasted_iota(jnp.int32, (SLOT, 128), 1)
    for quarter in range(4):
        blocks = [got[8 * quarter + k].astype(F32) for k in range(8)]
        for bit in range(3):
            width = 16 << bit
            low_side = (lane & width) == 0
            for k in range(8):
                if not k & (1 << bit):
                    a, b = blocks[k], blocks[k | (1 << bit)]
                    blocks[k] = jnp.where(low_side, a, pltpu.roll(b, width, 1))
                    blocks[k | (1 << bit)] = jnp.where(low_side, pltpu.roll(a, 128 - width, 1), b)
        stack = jnp.concatenate(blocks, axis=0).astype(BF16)
        straight = dot(unpack[...], stack)
        for piece in range(3):
            at = (3 * quarter + piece) * 128
            for f, ref in enumerate((x_ref, g_ref, n_ref)):
                row = 72 * f + 24 * piece
                ref[:, at : at + 128] = straight[row : row + 24]

    def quarters(x):
        return [x[:, k * QUARTER : (k + 1) * QUARTER] for k in range(4)]

    def analyse(field):
        q0, q1, q2, q3 = quarters(x_ref[...] * field)
        even, odd = q0 + q2, q1 + q3
        found = [
            dot3(even + odd, t0),
            dot3(even - odd, t2),
            dot3(jnp.concatenate([q0 - q2, q1 - q3], axis=1), t1),
        ]
        return jnp.concatenate(found, axis=1) * spectrum

    def synthesize(coeffs):
        scaled = coeffs * spectrum
        e0 = dot3(scaled[:, :128], b0)
        e2 = dot3(scaled[:, 128:256], b2)
        o = dot3(scaled[:, 256:], b1)
        oa, ob = o[:, :QUARTER], o[:, QUARTER:]
        plus, minus = e0 + e2, e0 - e2
        line = jnp.concatenate([plus + oa, minus + ob, plus - oa, minus - ob], axis=1)
        seen = (x_ref[...] * line).reshape(LINES, MEMBERS, NLON)
        total = jnp.sum(seen, axis=1, keepdims=True)
        return jnp.broadcast_to(total, (LINES, MEMBERS, NLON)).reshape(LINES * MEMBERS, NLON)

    def send_coeffs(v, coeffs):
        c_ref[...] = coeffs
        for k in range(N_MEM):
            for m in range(2):
                for s in range(LINES):
                    out_c[v, k, m * LINES + s : m * LINES + s + 1, :] = c_ref[s * 8 + 2 * k + m : s * 8 + 2 * k + m + 1, :]
        for d in (2, 3, 1):
            peer = mem_peer(d)
            pltpu.make_async_remote_copy(
                out_c.at[v, peer["mem"]], in_c.at[v, mem], send_c.at[v], recv_c.at[v], device_id=peer, device_id_type=MESH
            ).start()
        in_c[v, mem] = out_c[v, mem]

    def total_of(x):
        return jnp.sum(x, keepdims=True)

    f0 = g_ref[...]
    coeffs = analyse(f0)
    send_coeffs(0, coeffs)
    u0 = synthesize(coeffs)
    f1 = n_ref[...] * u0
    m1, m2 = total_of(f0 * u0), total_of(f1 * u0)
    coeffs = analyse(f1)
    send_coeffs(1, coeffs)
    u1 = synthesize(coeffs)
    f2 = n_ref[...] * u1
    m3, m4 = total_of(f1 * u1), total_of(f2 * u1)

    place = lax.broadcasted_iota(jnp.int32, (1, 128), 1)
    own = jnp.zeros((1, 128), F32)
    for k, value in enumerate((m1, m2, m3, m4)):
        own = jnp.where(place == k, value, own)

    def send_sums(stage, part, sums, peer_of, index):
        @pl.loop(1, 32)
        def _(d):
            pltpu.make_async_remote_copy(
                part, sums.at[index], send_s.at[stage], recv_s.at[stage], device_id=peer_of(d), device_id_type=MESH
            ).start()

    def wait_sums(stage, sums):
        lots = sums.at[pl.ds(0, 31)]
        pltpu.make_async_copy(lots, lots, recv_s.at[stage]).wait()
        return jnp.sum(sums[...], axis=0)

    part1[...] = own
    send_sums(0, part1, sums1, lon_peer, lon)
    sums1[lon] = own
    send_coeffs(2, analyse(f2))
    own = wait_sums(0, sums1)
    part2[...] = own
    send_sums(1, part2, sums2, group_peer, group)
    sums2[group] = own
    three = in_c.at[0, pl.ds(0, 3)]
    for v in range(3):
        pltpu.make_async_copy(three, three, recv_c.at[v]).wait()
    v0, v1, v2 = (in_c[v].reshape(32, 512) for v in range(3))
    moments = wait_sums(1, sums2)
    m1, m2, m3, m4 = (total_of(jnp.where(place == k, moments, 0.0)) for k in range(4))

    step = m1 / (m1 + m2)
    rest = 1.0 - step
    norm = rest * rest * m1 - 2.0 * step * rest * m2 + step * step * m3
    growth = norm / m1
    a = rest + growth
    curved = a * a * (m1 + m2) - 2.0 * a * step * (m2 + m3) + step * step * (m3 + m4)
    step_next = norm / curved
    found = (step + step_next * a) * v0 - (step_next * step) * v1
    left = (rest - step_next * a) * v0 - (step + step_next * (a - step)) * v1 + (step_next * step) * v2
    high, low = split(jnp.concatenate([found, left], axis=0))
    both = dot(jnp.concatenate([high, low], axis=0), order[...])
    last[...] = (both[:64] + both[64:]).reshape(8, 8, 512)
    for m in range(2):
        for s in range(LINES):
            for k in range(N_MEM):
                row = LINES * m + s
                sol_ref[m, s, k : k + 1, :] = last[k, row : row + 1, :]
                res_ref[m, s, k : k + 1, :] = last[N_MEM + k, row : row + 1, :]

    three = mine.at[pl.ds(0, 3)]
    pltpu.make_async_copy(three, three, send_a).wait()
    lots = got.at[pl.ds(0, 31)]
    pltpu.make_async_copy(lots, lots, send_b).wait()
    three = in_c.at[0, pl.ds(0, 3)]
    for v in range(3):
        pltpu.make_async_copy(three, three, send_c.at[v]).wait()
    for stage, sums in enumerate((sums1, sums2)):
        lots = sums.at[pl.ds(0, 31)]
        pltpu.make_async_copy(lots, lots, send_s.at[stage]).wait()


def body(perturbations, innovation, obs_weight, obs_cell, obs_level, cutoff):
    consts = [jnp.asarray(c) for c in constants()]
    vmem = pl.BlockSpec(memory_space=pltpu.VMEM)
    anywhere = pl.BlockSpec(memory_space=pl.ANY)
    out = jax.ShapeDtypeStruct((2, LINES, N_MEM, 2 * KMAX), F32)
    dma = pltpu.SemaphoreType.DMA
    obs = (innovation, obs_weight, obs_cell, obs_level)
    scratch = [pltpu.VMEM(c.shape, c.dtype) for c in (*obs, *consts)] + [
        pltpu.VMEM((N_MEM, 2, COLS, ROWS), BF16),
        pltpu.VMEM((N_LON, SLOT, 128), BF16),
        pltpu.VMEM((N_LON, SLOT, 128), BF16),
        pltpu.VMEM((24, NLON), F32),
        pltpu.VMEM((24, NLON), F32),
        pltpu.VMEM((24, NLON), F32),
        pltpu.VMEM((24, 512), F32),
        pltpu.VMEM((3, 4, 8, 512), F32),
        pltpu.VMEM((3, 4, 8, 512), F32),
        pltpu.VMEM((1, 128), F32),
        pltpu.VMEM((32, 1, 128), F32),
        pltpu.VMEM((1, 128), F32),
        pltpu.VMEM((32, 1, 128), F32),
        pltpu.VMEM((8, 8, 512), F32),
        dma((len(obs) + len(consts) + 1,)),
        dma,
        dma,
        dma,
        dma,
        dma((3,)),
        dma((3,)),
        dma((2,)),
        dma((2,)),
    ]
    found, left = pl.pallas_call(
        kernel,
        out_shape=(out, out),
        in_specs=[anywhere] * 5 + [pl.BlockSpec(memory_space=pltpu.SMEM)] + [anywhere] * len(consts),
        out_specs=(vmem, vmem),
        scratch_shapes=scratch,
        compiler_params=pltpu.CompilerParams(
            collective_id=0, has_side_effects=True, vmem_limit_bytes=62 * 1024 * 1024
        ),
    )(jnp.swapaxes(perturbations, 2, 3), *obs, cutoff, *consts)
    return jnp.swapaxes(found, 1, 2), jnp.swapaxes(left, 1, 2)


def solution(mesh):
    in_specs = (
        P("mem", None, "lat", "lon"),
        P("lat", "lon"),
        P("lat", "lon"),
        P("lat", "lon"),
        P("lat", "lon"),
        P(),
    )
    out_specs = (P("mem", None, ("lat", "lon"), None), P("mem", None, ("lat", "lon"), None))
    return jax.shard_map(body, mesh=mesh, in_specs=in_specs, out_specs=out_specs, check_vma=False)
```

```python
import jax
import jax.numpy as jnp
import ml_dtypes
import numpy as np
from jax import lax
from jax.experimental import pallas as pl
from jax.experimental.pallas import tpu as pltpu
from jax.sharding import PartitionSpec as P

MESH = pl.DeviceIdType.MESH
BF16 = jnp.bfloat16
F32 = jnp.float32
NLON = 1536
KMAX = 256
MEMBERS = 8
N_MEM = 4
N_LAT = 8
N_LON = 32
ROWS = 96
COLS = 48
LINES = 3
QUARTER = NLON // 4
SLOT = 16


def farthest_first(first, second, hops):
    steps = [(i, j) for i in range(first) for j in range(second) if i or j]
    return sorted(steps, key=lambda step: -hops(*step))


FAR_LON = farthest_first(8, 4, lambda i, j: min(i, 8 - i) + 2 * min(j, 4 - j))
FAR_GROUP = farthest_first(4, 8, lambda i, j: min(j, 8 - j) + (i > 0))


def halves(table):
    high = table.astype(ml_dtypes.bfloat16)
    low = (table - high.astype(np.float64)).astype(ml_dtypes.bfloat16)
    return np.stack([high, low])


def constants():
    piece, source, i = np.meshgrid(np.arange(3), np.arange(8), np.arange(16), indexing="ij")
    column = (48 * source + 16 * piece + i).reshape(-1)

    def table(columns, cosines, sines):
        angle = 2.0 * np.pi / NLON
        cos = np.cos((columns[:, None] * cosines[None] % NLON) * angle)
        sin = np.sin((columns[:, None] * sines[None] % NLON) * angle)
        return np.concatenate([cos, sin], axis=1) / 16.0

    c0, s0 = np.arange(0, 256, 4), np.arange(4, 257, 4)
    c2 = np.arange(2, 256, 4)
    c1 = np.arange(1, 256, 2)
    t0 = table(column, c0, s0)
    t2 = table(column, c2, c2)
    t1 = table(np.concatenate([column, QUARTER + column]), c1, c1)
    wave = np.concatenate([c0, s0, c2, c2, c1, c1])
    natural = np.concatenate([c0, 255 + s0, c2, 255 + c2, c1, 255 + c1])
    order = np.zeros((512, 512))
    order[np.arange(512), natural] = 1

    pack = np.zeros((5, N_LON * SLOT, ROWS))
    unpack = np.zeros((216, 128))
    for s in range(LINES):
        for u in range(5):
            peer = np.arange(N_LON)
            pack[u, peer * SLOT + 3 * u + s, 3 * peer + s] = 1
        for piece in range(3):
            for m in range(MEMBERS):
                row = piece * 24 + s * 8 + m
                unpack[row, m * SLOT + piece * 3 + s] = 1
                for f in range(2):
                    for h in range(2):
                        r = (9, 12, 9)[piece] + s
                        q = (0, 0, 4)[piece] + 2 * f + h
                        unpack[72 * (f + 1) + row, q * SLOT + r] = 1
    small = [a.astype(ml_dtypes.bfloat16) for a in (pack, unpack)]
    tables = [halves(t) for t in (t0, t2, t1, t0.T, t2.T, t1.T)]
    return small + tables + [order.astype(ml_dtypes.bfloat16), np.broadcast_to(wave, (8, 512)).astype(np.float32)]


def dot(a, b):
    return jnp.dot(a, b, preferred_element_type=F32)


def dot_nt(a, b):
    return lax.dot_general(a, b, (((1,), (1,)), ((), ())), preferred_element_type=F32)


def split(x):
    high = x.astype(BF16)
    return high, (x - high.astype(F32)).astype(BF16)


def dot3(x, table):
    high, low = split(x)
    both = dot(jnp.concatenate([high, low], axis=0), table[0])
    n = x.shape[0]
    return both[:n] + (both[n:] + dot(high, table[1]))


def kernel(p_ref, inn_in, wt_in, cell_in, lev_in, cut_ref, *refs):
    n_const = 10
    loads_in = (inn_in, wt_in, cell_in, lev_in) + refs[:n_const]
    sol_ref, res_ref = refs[n_const : n_const + 2]
    scratch = refs[n_const + 2 :]
    n_load = n_const + 4
    loads_ref = scratch[:n_load]
    (mine, packed, got, x_ref, g_ref, n_ref, c_ref, out_c, in_c, part1, sums1, part2, sums2, last) = scratch[n_load : n_load + 14]
    load_sem, send_a, recv_a, send_b, recv_b, send_c, recv_c, send_s, recv_s = scratch[n_load + 14 :]
    inn_ref, wt_ref, cell_ref, lev_ref, pack, unpack, t0, t2, t1, b0, b2, b1, order, wave = loads_ref

    mem, lat, lon = lax.axis_index("mem"), lax.axis_index("lat"), lax.axis_index("lon")
    group = mem * N_LAT + lat

    depth, side = lon // 4, lax.rem(lon, 4)

    def lon_peer(d):
        return {"mem": mem, "lat": lat, "lon": lax.rem(depth + d[0], 8) * 4 + lax.rem(side + d[1], 4)}

    def group_peer(d):
        return {"mem": lax.rem(mem + d[0], N_MEM), "lat": lax.rem(lat + d[1], N_LAT), "lon": lon}

    def mem_peer(d):
        return {"mem": lax.rem(mem + d, N_MEM), "lat": lat, "lon": lon}

    barrier = pltpu.get_barrier_semaphore()

    for d in FAR_LON:
        pl.semaphore_signal(barrier, inc=1, device_id=lon_peer(d), device_id_type=MESH)
    for d in FAR_GROUP:
        pl.semaphore_signal(barrier, inc=1, device_id=group_peer(d), device_id_type=MESH)

    loads = [pltpu.make_async_copy(loads_in[k], loads_ref[k], load_sem.at[k]) for k in range(n_load)]
    for copy in loads:
        copy.start()
    own_members = pltpu.make_async_copy(p_ref.at[:, mem], mine.at[mem], load_sem.at[n_load])
    own_members.start()

    out_c[...] = jnp.zeros_like(out_c)

    pl.semaphore_wait(barrier, 62)

    for d in (2, 3, 1):
        peer = mem_peer(d)
        pltpu.make_async_remote_copy(
            p_ref.at[:, peer["mem"]], mine.at[mem], send_a, recv_a, device_id=peer, device_id_type=MESH
        ).start()

    for k in range(4):
        loads[k].wait()
    cell = cell_ref[...].astype(F32)
    row_of = jnp.floor((cell + 0.5) * (1.0 / COLS))
    col_of = cell - COLS * row_of
    key = row_of + ROWS * lev_ref[...].astype(F32)
    rows = lax.broadcasted_iota(jnp.int32, (ROWS, 1), 0) + ROWS * mem
    row_hot = jnp.where(rows.astype(F32) == key, 1.0, 0.0).astype(BF16)
    weight = wt_ref[...]
    col_hit = lax.broadcasted_iota(jnp.int32, (COLS, 1), 0).astype(F32) == col_of
    tile = jnp.zeros((2 * COLS, ROWS), F32)
    parts = [split(weight * inn_ref[...]), split(weight)]
    for h in range(2):
        placed = jnp.concatenate([jnp.where(col_hit, part[h].astype(F32), 0.0) for part in parts], axis=0).astype(BF16)
        tile += dot_nt(placed, row_hot)
    tiles = split(tile)

    def of_fields(piece):
        return [tiles[h][f * COLS + piece * 16 : f * COLS + piece * 16 + 16] for f in range(2) for h in range(2)]

    nothing = jnp.zeros((64, ROWS), BF16)
    chunks = [jnp.concatenate(of_fields(0) + of_fields(2), axis=0), jnp.concatenate(of_fields(1) + [nothing], axis=0)]
    loads[4].wait()
    message = dot_nt(pack[3], chunks[0]) + dot_nt(pack[4], chunks[1])

    own_members.wait()
    three = mine.at[pl.ds(0, 3)]
    pltpu.make_async_copy(three, three, recv_a).wait()
    for piece in range(3):
        chunk = [mine[k, a, piece * 16 : piece * 16 + 16, :] for k in range(N_MEM) for a in range(2)]
        message += dot_nt(pack[piece], jnp.concatenate(chunk, axis=0))
    packed[...] = message.astype(BF16).reshape(N_LON, SLOT, 128)

    for d in FAR_LON:
        peer = lon_peer(d)
        pltpu.make_async_remote_copy(
            packed.at[peer["lon"]], got.at[lon], send_b, recv_b, device_id=peer, device_id_type=MESH
        ).start()

    got[lon] = packed[lon]
    for copy in loads[5:]:
        copy.wait()
    cutoff = cut_ref[mem].astype(F32)
    scaled = wave[0:1, :] / cutoff
    spectrum = 1.0 / (1.0 + scaled * scaled)
    lots = got.at[pl.ds(0, 31)]
    pltpu.make_async_copy(lots, lots, recv_b).wait()

    lane = lax.broadcasted_iota(jnp.int32, (SLOT, 128), 1)
    for quarter in range(4):
        blocks = [got[8 * quarter + k].astype(F32) for k in range(8)]
        for bit in range(3):
            width = 16 << bit
            low_side = (lane & width) == 0
            for k in range(8):
                if not k & (1 << bit):
                    a, b = blocks[k], blocks[k | (1 << bit)]
                    blocks[k] = jnp.where(low_side, a, pltpu.roll(b, width, 1))
                    blocks[k | (1 << bit)] = jnp.where(low_side, pltpu.roll(a, 128 - width, 1), b)
        stack = jnp.concatenate(blocks, axis=0).astype(BF16)
        straight = dot(unpack[...], stack)
        for piece in range(3):
            at = (3 * quarter + piece) * 128
            for f, ref in enumerate((x_ref, g_ref, n_ref)):
                row = 72 * f + 24 * piece
                ref[:, at : at + 128] = straight[row : row + 24]

    def quarters(x):
        return [x[:, k * QUARTER : (k + 1) * QUARTER] for k in range(4)]

    def analyse(field):
        q0, q1, q2, q3 = quarters(x_ref[...] * field)
        even, odd = q0 + q2, q1 + q3
        found = [
            dot3(even + odd, t0),
            dot3(even - odd, t2),
            dot3(jnp.concatenate([q0 - q2, q1 - q3], axis=1), t1),
        ]
        return jnp.concatenate(found, axis=1) * spectrum

    def synthesize(coeffs):
        scaled = coeffs * spectrum
        e0 = dot3(scaled[:, :128], b0)
        e2 = dot3(scaled[:, 128:256], b2)
        o = dot3(scaled[:, 256:], b1)
        oa, ob = o[:, :QUARTER], o[:, QUARTER:]
        plus, minus = e0 + e2, e0 - e2
        line = jnp.concatenate([plus + oa, minus + ob, plus - oa, minus - ob], axis=1)
        seen = (x_ref[...] * line).reshape(LINES, MEMBERS, NLON)
        total = jnp.sum(seen, axis=1, keepdims=True)
        return jnp.broadcast_to(total, (LINES, MEMBERS, NLON)).reshape(LINES * MEMBERS, NLON)

    def send_coeffs(v, coeffs):
        c_ref[...] = coeffs
        for k in range(N_MEM):
            for m in range(2):
                for s in range(LINES):
                    out_c[v, k, m * LINES + s : m * LINES + s + 1, :] = c_ref[s * 8 + 2 * k + m : s * 8 + 2 * k + m + 1, :]
        for d in (2, 3, 1):
            peer = mem_peer(d)
            pltpu.make_async_remote_copy(
                out_c.at[v, peer["mem"]], in_c.at[v, mem], send_c.at[v], recv_c.at[v], device_id=peer, device_id_type=MESH
            ).start()
        in_c[v, mem] = out_c[v, mem]

    def total_of(x):
        return jnp.sum(x, keepdims=True)

    f0 = g_ref[...]
    coeffs = analyse(f0)
    send_coeffs(0, coeffs)
    u0 = synthesize(coeffs)
    f1 = n_ref[...] * u0
    m1, m2 = total_of(f0 * u0), total_of(f1 * u0)
    coeffs = analyse(f1)
    send_coeffs(1, coeffs)
    u1 = synthesize(coeffs)
    f2 = n_ref[...] * u1
    m3, m4 = total_of(f1 * u1), total_of(f2 * u1)

    place = lax.broadcasted_iota(jnp.int32, (1, 128), 1)
    own = jnp.zeros((1, 128), F32)
    for k, value in enumerate((m1, m2, m3, m4)):
        own = jnp.where(place == k, value, own)

    def send_sums(stage, part, sums, peer_of, index):
        for d in (FAR_LON, FAR_GROUP)[stage]:
            pltpu.make_async_remote_copy(
                part, sums.at[index], send_s.at[stage], recv_s.at[stage], device_id=peer_of(d), device_id_type=MESH
            ).start()

    def wait_sums(stage, sums):
        lots = sums.at[pl.ds(0, 31)]
        pltpu.make_async_copy(lots, lots, recv_s.at[stage]).wait()
        return jnp.sum(sums[...], axis=0)

    part1[...] = own
    send_sums(0, part1, sums1, lon_peer, lon)
    sums1[lon] = own
    send_coeffs(2, analyse(f2))
    own = wait_sums(0, sums1)
    part2[...] = own
    send_sums(1, part2, sums2, group_peer, group)
    sums2[group] = own
    three = in_c.at[0, pl.ds(0, 3)]
    for v in range(3):
        pltpu.make_async_copy(three, three, recv_c.at[v]).wait()
    v0, v1, v2 = (in_c[v].reshape(32, 512) for v in range(3))
    moments = wait_sums(1, sums2)
    m1, m2, m3, m4 = (total_of(jnp.where(place == k, moments, 0.0)) for k in range(4))

    step = m1 / (m1 + m2)
    rest = 1.0 - step
    norm = rest * rest * m1 - 2.0 * step * rest * m2 + step * step * m3
    growth = norm / m1
    a = rest + growth
    curved = a * a * (m1 + m2) - 2.0 * a * step * (m2 + m3) + step * step * (m3 + m4)
    step_next = norm / curved
    found = (step + step_next * a) * v0 - (step_next * step) * v1
    left = (rest - step_next * a) * v0 - (step + step_next * (a - step)) * v1 + (step_next * step) * v2
    high, low = split(jnp.concatenate([found, left], axis=0))
    both = dot(jnp.concatenate([high, low], axis=0), order[...])
    last[...] = (both[:64] + both[64:]).reshape(8, 8, 512)
    for m in range(2):
        for s in range(LINES):
            for k in range(N_MEM):
                row = LINES * m + s
                sol_ref[m, s, k : k + 1, :] = last[k, row : row + 1, :]
                res_ref[m, s, k : k + 1, :] = last[N_MEM + k, row : row + 1, :]

    three = mine.at[pl.ds(0, 3)]
    pltpu.make_async_copy(three, three, send_a).wait()
    lots = got.at[pl.ds(0, 31)]
    pltpu.make_async_copy(lots, lots, send_b).wait()
    three = in_c.at[0, pl.ds(0, 3)]
    for v in range(3):
        pltpu.make_async_copy(three, three, send_c.at[v]).wait()
    for stage, sums in enumerate((sums1, sums2)):
        lots = sums.at[pl.ds(0, 31)]
        pltpu.make_async_copy(lots, lots, send_s.at[stage]).wait()


def body(perturbations, innovation, obs_weight, obs_cell, obs_level, cutoff):
    consts = [jnp.asarray(c) for c in constants()]
    vmem = pl.BlockSpec(memory_space=pltpu.VMEM)
    anywhere = pl.BlockSpec(memory_space=pl.ANY)
    out = jax.ShapeDtypeStruct((2, LINES, N_MEM, 2 * KMAX), F32)
    dma = pltpu.SemaphoreType.DMA
    obs = (innovation, obs_weight, obs_cell, obs_level)
    scratch = [pltpu.VMEM(c.shape, c.dtype) for c in (*obs, *consts)] + [
        pltpu.VMEM((N_MEM, 2, COLS, ROWS), BF16),
        pltpu.VMEM((N_LON, SLOT, 128), BF16),
        pltpu.VMEM((N_LON, SLOT, 128), BF16),
        pltpu.VMEM((24, NLON), F32),
        pltpu.VMEM((24, NLON), F32),
        pltpu.VMEM((24, NLON), F32),
        pltpu.VMEM((24, 512), F32),
        pltpu.VMEM((3, 4, 8, 512), F32),
        pltpu.VMEM((3, 4, 8, 512), F32),
        pltpu.VMEM((1, 128), F32),
        pltpu.VMEM((32, 1, 128), F32),
        pltpu.VMEM((1, 128), F32),
        pltpu.VMEM((32, 1, 128), F32),
        pltpu.VMEM((8, 8, 512), F32),
        dma((len(obs) + len(consts) + 1,)),
        dma,
        dma,
        dma,
        dma,
        dma((3,)),
        dma((3,)),
        dma((2,)),
        dma((2,)),
    ]
    found, left = pl.pallas_call(
        kernel,
        out_shape=(out, out),
        in_specs=[anywhere] * 5 + [pl.BlockSpec(memory_space=pltpu.SMEM)] + [anywhere] * len(consts),
        out_specs=(vmem, vmem),
        scratch_shapes=scratch,
        compiler_params=pltpu.CompilerParams(
            collective_id=0, has_side_effects=True, vmem_limit_bytes=60 * 1024 * 1024
        ),
    )(jnp.swapaxes(perturbations, 2, 3), *obs, cutoff, *consts)
    return jnp.swapaxes(found, 1, 2), jnp.swapaxes(left, 1, 2)


def solution(mesh):
    in_specs = (
        P("mem", None, "lat", "lon"),
        P("lat", "lon"),
        P("lat", "lon"),
        P("lat", "lon"),
        P("lat", "lon"),
        P(),
    )
    out_specs = (P("mem", None, ("lat", "lon"), None), P("mem", None, ("lat", "lon"), None))
    return jax.shard_map(body, mesh=mesh, in_specs=in_specs, out_specs=out_specs, check_vma=False)
```

```python
import jax
import jax.numpy as jnp
import ml_dtypes
import numpy as np
from jax import lax
from jax.experimental import pallas as pl
from jax.experimental.pallas import tpu as pltpu
from jax.sharding import PartitionSpec as P

MESH = pl.DeviceIdType.MESH
BF16 = jnp.bfloat16
F32 = jnp.float32
NLON = 1536
KMAX = 256
MEMBERS = 8
N_MEM = 4
N_LAT = 8
N_LON = 32
ROWS = 96
COLS = 48
LINES = 3
QUARTER = NLON // 4


def farthest_first(first, second, hops):
    steps = [(i, j) for i in range(first) for j in range(second) if i or j]
    return sorted(steps, key=lambda step: -hops(*step))


FAR_LON = farthest_first(8, 4, lambda i, j: min(i, 8 - i) + 2 * min(j, 4 - j))
FAR_ALL = sorted(
    [(k, *step) for k in range(4) for step in [(0, 0), *FAR_LON] if k or any(step)],
    key=lambda step: -(min(step[1], 8 - step[1]) + 2 * min(step[2], 4 - step[2]) + (step[0] > 0)),
)
FAR_LAT = (4, 3, 5, 2, 6, 1, 7)


def halves(table):
    high = table.astype(ml_dtypes.bfloat16)
    low = (table - high.astype(np.float64)).astype(ml_dtypes.bfloat16)
    return np.stack([high, low])


def constants():
    piece, source, i = np.meshgrid(np.arange(3), np.arange(8), np.arange(16), indexing="ij")
    column = (48 * source + 16 * piece + i).reshape(-1)

    def table(columns, cosines, sines):
        angle = 2.0 * np.pi / NLON
        cos = np.cos((columns[:, None] * cosines[None] % NLON) * angle)
        sin = np.sin((columns[:, None] * sines[None] % NLON) * angle)
        return np.concatenate([cos, sin], axis=1) / 16.0

    c0, s0 = np.arange(0, 256, 4), np.arange(4, 257, 4)
    c2 = np.arange(2, 256, 4)
    c1 = np.arange(1, 256, 2)
    t0 = table(column, c0, s0)
    t2 = table(column, c2, c2)
    t1 = table(np.concatenate([column, QUARTER + column]), c1, c1)
    wave = np.concatenate([c0, s0, c2, c2, c1, c1])
    natural = np.concatenate([c0, 255 + s0, c2, 255 + c2, c1, 255 + c1])
    order = np.zeros((512, 512))
    order[np.arange(512), natural] = 1

    lines = np.zeros((288, 288))
    fields = np.zeros((2, 288, 2, 96))
    for quarter in range(4):
        for piece in range(3):
            for s in range(LINES):
                for m in range(MEMBERS):
                    row = (quarter * 3 + piece) * 24 + s * 8 + m
                    lines[row, ((m % 2) * 3 + piece) * 48 + (m // 2) * 12 + quarter * 3 + s] = 1
                    for f in range(2):
                        k, q = divmod(3 * f + piece, 2)
                        fields[f, row, :, q * 48 + k * 12 + quarter * 3 + s] = 1
    small = [a.astype(ml_dtypes.bfloat16) for a in (lines, fields.reshape(576, 192))]
    tables = [halves(t) for t in (t0, t2, t1, t0.T, t2.T, t1.T)]
    return small + tables + [order.astype(ml_dtypes.bfloat16), np.broadcast_to(wave, (8, 512)).astype(np.float32)]


def dot(a, b):
    return jnp.dot(a, b, preferred_element_type=F32)


def dot_nt(a, b):
    return lax.dot_general(a, b, (((1,), (1,)), ((), ())), preferred_element_type=F32)


def split(x):
    high = x.astype(BF16)
    return high, (x - high.astype(F32)).astype(BF16)


def dot3(x, table):
    high, low = split(x)
    both = dot(jnp.concatenate([high, low], axis=0), table[0])
    n = x.shape[0]
    return both[:n] + (both[n:] + dot(high, table[1]))


def kernel(p_ref, inn_in, wt_in, cell_in, lev_in, cut_ref, *refs):
    n_const = 10
    loads_in = (inn_in, wt_in, cell_in, lev_in, p_ref) + refs[:n_const]
    sets_ref, *factor_refs = refs[n_const : n_const + 3]
    scratch = refs[n_const + 3 :]
    n_load = n_const + 5
    loads_ref = scratch[:n_load]
    (packed, got, x_ref, g_ref, n_ref, c_ref, out_c, in_c, part1, sums1, part2, sums2, last, sets) = scratch[n_load : n_load + 14]
    load_sem, send_b, recv_b, send_c, recv_c, send_s, recv_s = scratch[n_load + 14 :]
    inn_ref, wt_ref, cell_ref, lev_ref, p_vmem, to_lines, to_fields, t0, t2, t1, b0, b2, b1, order, wave = loads_ref

    mem, lat, lon = lax.axis_index("mem"), lax.axis_index("lat"), lax.axis_index("lon")

    depth, side = lon // 4, lax.rem(lon, 4)

    def lat_peer(d):
        return {"mem": mem, "lat": lax.rem(lat + d, N_LAT), "lon": lon}

    def mem_peer(d):
        return {"mem": lax.rem(mem + d, N_MEM), "lat": lat, "lon": lon}

    def line_peer(d):
        return {
            "mem": lax.rem(mem + d[0], N_MEM),
            "lat": lat,
            "lon": lax.rem(depth + d[1], 8) * 4 + lax.rem(side + d[2], 4),
        }

    barrier = pltpu.get_barrier_semaphore()

    loads = [pltpu.make_async_copy(loads_in[k], loads_ref[k], load_sem.at[k]) for k in range(n_load)]
    for copy in loads[:5]:
        copy.start()
    for d in FAR_ALL:
        pl.semaphore_signal(barrier, inc=1, device_id=line_peer(d), device_id_type=MESH)
    for d in FAR_LAT:
        pl.semaphore_signal(barrier, inc=1, device_id=lat_peer(d), device_id_type=MESH)

    for copy in loads[5:]:
        copy.start()
    out_c[...] = jnp.zeros_like(out_c)

    for k in range(5):
        loads[k].wait()
    cell = cell_ref[...].astype(F32)
    row_of = jnp.floor((cell + 0.5) * (1.0 / COLS))
    col_of = cell - COLS * row_of
    key = row_of + ROWS * lev_ref[...].astype(F32)
    rows = lax.broadcasted_iota(jnp.int32, (4 * ROWS, 1), 0)
    row_hot = jnp.where(rows.astype(F32) == key, 1.0, 0.0).astype(BF16)
    lane_row = lax.broadcasted_iota(jnp.int32, (32, 1), 0)
    share = 2 * mem + jnp.where(lane_row >= 16, 1, 0)
    field = jnp.where(share >= 3, 1, 0) + jnp.where(share >= 6, 1, 0)
    column = (share - 3 * field) * 16 + lane_row - jnp.where(lane_row >= 16, 16, 0)
    hit = column.astype(F32) == col_of
    weight = wt_ref[...]
    scaled_d, scaled_w = split(weight * inn_ref[...]), split(weight)
    blank = jnp.zeros((ROWS, 2048), BF16)
    tile = jnp.zeros((4 * ROWS, 128), F32)
    for h in range(2):
        value = jnp.where(field == 0, scaled_d[h].astype(F32), jnp.where(field == 1, scaled_w[h].astype(F32), 0.0))
        placed = jnp.where(hit, value, 0.0).astype(BF16)
        tile += dot_nt(row_hot, jnp.concatenate([blank, placed], axis=0))
    same = lax.broadcasted_iota(jnp.int32, (ROWS, ROWS), 0) == lax.broadcasted_iota(jnp.int32, (ROWS, ROWS), 1)
    eye = jnp.where(same, 1.0, 0.0).astype(BF16)
    for k in range(N_MEM):
        both = jnp.concatenate([p_vmem[0, k], p_vmem[1, k], jnp.zeros((32, ROWS), BF16)], axis=0)
        message = dot_nt(eye, both) + tile[k * ROWS : (k + 1) * ROWS]
        packed[k] = message.reshape(N_LON, LINES, 1, 128)

    pl.semaphore_wait(barrier, 134)

    place_here = (lax.rem(lon, 8) * 4 + mem) * 4 + lon // 8
    for d in FAR_ALL:
        peer = line_peer(d)
        pltpu.make_async_remote_copy(
            packed.at[peer["mem"], peer["lon"]], got.at[place_here], send_b, recv_b, device_id=peer, device_id_type=MESH
        ).start()

    got[place_here] = packed[mem, lon]
    for copy in loads[5:]:
        copy.wait()
    cutoff = cut_ref[mem].astype(F32)
    scaled = wave[0:1, :] / cutoff
    spectrum = 1.0 / (1.0 + scaled * scaled)
    lots = got.at[pl.ds(0, 127)]
    pltpu.make_async_copy(lots, lots, recv_b).wait()

    lane = lax.broadcasted_iota(jnp.int32, (48, 128), 1)
    blocks = [got[16 * k : 16 * k + 16].reshape(48, 128) for k in range(8)]
    for bit in range(3):
        width = 16 << bit
        low_side = (lane & width) == 0
        for k in range(8):
            if not k & (1 << bit):
                a, b = blocks[k], blocks[k | (1 << bit)]
                blocks[k] = jnp.where(low_side, a, pltpu.roll(b, width, 1))
                blocks[k | (1 << bit)] = jnp.where(low_side, pltpu.roll(a, 128 - width, 1), b)
    x_all = dot(to_lines[...], jnp.concatenate(blocks[:6], axis=0).astype(BF16))
    f_all = dot(to_fields[...], jnp.concatenate(split(jnp.concatenate(blocks[6:], axis=0)), axis=0))
    for t in range(12):
        x_ref[:, t * 128 : t * 128 + 128] = x_all[t * 24 : t * 24 + 24]
        g_ref[:, t * 128 : t * 128 + 128] = f_all[t * 24 : t * 24 + 24]
        n_ref[:, t * 128 : t * 128 + 128] = f_all[288 + t * 24 : 288 + t * 24 + 24]

    def quarters(x):
        return [x[:, k * QUARTER : (k + 1) * QUARTER] for k in range(4)]

    def analyse(field):
        q0, q1, q2, q3 = quarters(x_ref[...] * field)
        even, odd = q0 + q2, q1 + q3
        found = [
            dot3(even + odd, t0),
            dot3(even - odd, t2),
            dot3(jnp.concatenate([q0 - q2, q1 - q3], axis=1), t1),
        ]
        return jnp.concatenate(found, axis=1) * spectrum

    def synthesize(coeffs):
        scaled = coeffs * spectrum
        e0 = dot3(scaled[:, :128], b0)
        e2 = dot3(scaled[:, 128:256], b2)
        o = dot3(scaled[:, 256:], b1)
        oa, ob = o[:, :QUARTER], o[:, QUARTER:]
        plus, minus = e0 + e2, e0 - e2
        line = jnp.concatenate([plus + oa, minus + ob, plus - oa, minus - ob], axis=1)
        seen = (x_ref[...] * line).reshape(LINES, MEMBERS, NLON)
        total = jnp.sum(seen, axis=1, keepdims=True)
        return jnp.broadcast_to(total, (LINES, MEMBERS, NLON)).reshape(LINES * MEMBERS, NLON)

    def send_coeffs(v, coeffs):
        c_ref[...] = coeffs
        for k in range(N_MEM):
            for m in range(2):
                for s in range(LINES):
                    out_c[v, k, m * LINES + s : m * LINES + s + 1, :] = c_ref[s * 8 + 2 * k + m : s * 8 + 2 * k + m + 1, :]
        for d in (2, 3, 1):
            peer = mem_peer(d)
            pltpu.make_async_remote_copy(
                out_c.at[v, peer["mem"]], in_c.at[v, mem], send_c.at[v], recv_c.at[v], device_id=peer, device_id_type=MESH
            ).start()
        in_c[v, mem] = out_c[v, mem]

    def total_of(x):
        return jnp.sum(x, keepdims=True)

    f0 = g_ref[...]
    coeffs = analyse(f0)
    send_coeffs(0, coeffs)
    u0 = synthesize(coeffs)
    f1 = n_ref[...] * u0
    m1, m2 = total_of(f0 * u0), total_of(f1 * u0)
    coeffs = analyse(f1)
    send_coeffs(1, coeffs)
    u1 = synthesize(coeffs)
    f2 = n_ref[...] * u1
    m3, m4 = total_of(f1 * u1), total_of(f2 * u1)

    place = lax.broadcasted_iota(jnp.int32, (1, 128), 1)
    own = jnp.zeros((1, 128), F32)
    for k, value in enumerate((m1, m2, m3, m4)):
        own = jnp.where(place == k, value, own)

    def send_sums(stage, part, sums, peer_of, index):
        for d in (FAR_ALL, FAR_LAT)[stage]:
            pltpu.make_async_remote_copy(
                part, sums.at[index], send_s.at[stage], recv_s.at[stage], device_id=peer_of(d), device_id_type=MESH
            ).start()

    def wait_sums(stage, sums):
        lots = sums.at[pl.ds(0, sums.shape[0] - 1)]
        pltpu.make_async_copy(lots, lots, recv_s.at[stage]).wait()
        return jnp.sum(sums[...], axis=0)

    part1[...] = own
    send_sums(0, part1, sums1, line_peer, mem * N_LON + lon)
    sums1[mem * N_LON + lon] = own
    send_coeffs(2, analyse(f2))
    own = wait_sums(0, sums1)
    part2[...] = own
    send_sums(1, part2, sums2, lat_peer, lat)
    sums2[lat] = own
    three = in_c.at[0, pl.ds(0, 3)]
    for v in range(3):
        pltpu.make_async_copy(three, three, recv_c.at[v]).wait()
    for v in range(3):
        both = dot(jnp.concatenate(split(in_c[v].reshape(32, 512)), axis=0), order[...])
        last[...] = (both[:32] + both[32:]).reshape(N_MEM, 8, 512)
        for m in range(2):
            for s in range(LINES):
                for k in range(N_MEM):
                    sets[v, m, s, k : k + 1, :] = last[k, m * LINES + s : m * LINES + s + 1, :]
    sets_out = pltpu.make_async_copy(sets, sets_ref, load_sem.at[n_load])
    sets_out.start()
    moments = wait_sums(1, sums2)
    m1, m2, m3, m4 = (total_of(jnp.where(place == k, moments, 0.0)) for k in range(4))

    step = m1 / (m1 + m2)
    rest = 1.0 - step
    norm = rest * rest * m1 - 2.0 * step * rest * m2 + step * step * m3
    growth = norm / m1
    a = rest + growth
    curved = a * a * (m1 + m2) - 2.0 * a * step * (m2 + m3) + step * step * (m3 + m4)
    step_next = norm / curved
    factors = (
        step + step_next * a,
        -step_next * step,
        rest - step_next * a,
        -step - step_next * (a - step),
        step_next * step,
    )
    for k, factor in enumerate((*factors[:2], jnp.zeros((1, 1), F32), *factors[2:])):
        factor_refs[k // 3][k % 3 : k % 3 + 1, :] = jnp.broadcast_to(factor, (1, 512))
    sets_out.wait()

    lots = got.at[pl.ds(0, 127)]
    pltpu.make_async_copy(lots, lots, send_b).wait()
    three = in_c.at[0, pl.ds(0, 3)]
    for v in range(3):
        pltpu.make_async_copy(three, three, send_c.at[v]).wait()
    for stage, sums in enumerate((sums1, sums2)):
        lots = sums.at[pl.ds(0, sums.shape[0] - 1)]
        pltpu.make_async_copy(lots, lots, send_s.at[stage]).wait()


def body(perturbations, innovation, obs_weight, obs_cell, obs_level, cutoff):
    consts = [jnp.asarray(c) for c in constants()]
    vmem = pl.BlockSpec(memory_space=pltpu.VMEM)
    anywhere = pl.BlockSpec(memory_space=pl.ANY)
    sets_shape = jax.ShapeDtypeStruct((3, 2, LINES, N_MEM, 2 * KMAX), F32)
    factor_shape = jax.ShapeDtypeStruct((3, 2 * KMAX), F32)
    dma = pltpu.SemaphoreType.DMA
    obs = (innovation, obs_weight, obs_cell, obs_level)
    turned = jnp.swapaxes(perturbations, 2, 3)
    scratch = [pltpu.VMEM(c.shape, c.dtype) for c in (*obs, turned, *consts)] + [
        pltpu.VMEM((N_MEM, N_LON, LINES, 1, 128), F32),
        pltpu.VMEM((N_MEM * N_LON, LINES, 1, 128), F32),
        pltpu.VMEM((24, NLON), F32),
        pltpu.VMEM((24, NLON), F32),
        pltpu.VMEM((24, NLON), F32),
        pltpu.VMEM((24, 512), F32),
        pltpu.VMEM((3, 4, 8, 512), F32),
        pltpu.VMEM((3, 4, 8, 512), F32),
        pltpu.VMEM((1, 128), F32),
        pltpu.VMEM((N_MEM * N_LON, 1, 128), F32),
        pltpu.VMEM((1, 128), F32),
        pltpu.VMEM((N_LAT, 1, 128), F32),
        pltpu.VMEM((N_MEM, 8, 512), F32),
        pltpu.VMEM((3, 2, LINES, N_MEM, 512), F32),
        dma((len(obs) + 1 + len(consts) + 1,)),
        dma,
        dma,
        dma((3,)),
        dma((3,)),
        dma((2,)),
        dma((2,)),
    ]
    sets, *f = pl.pallas_call(
        kernel,
        out_shape=(sets_shape,) + (factor_shape,) * 2,
        in_specs=[anywhere] * 5 + [pl.BlockSpec(memory_space=pltpu.SMEM)] + [anywhere] * len(consts),
        out_specs=(anywhere,) + (vmem,) * 2,
        scratch_shapes=scratch,
        compiler_params=pltpu.CompilerParams(
            collective_id=0, has_side_effects=True, vmem_limit_bytes=60 * 1024 * 1024
        ),
    )(turned, *obs, cutoff, *consts)
    found, left = (jnp.sum(factor[:, None, None, None] * sets, axis=0) for factor in f)
    return jnp.swapaxes(found, 1, 2), jnp.swapaxes(left, 1, 2)


def solution(mesh):
    in_specs = (
        P("mem", None, "lat", "lon"),
        P("lat", "lon"),
        P("lat", "lon"),
        P("lat", "lon"),
        P("lat", "lon"),
        P(),
    )
    out_specs = (P("mem", None, ("lat", "lon"), None), P("mem", None, ("lat", "lon"), None))
    return jax.shard_map(body, mesh=mesh, in_specs=in_specs, out_specs=out_specs, check_vma=False)
```

```python
import jax
import jax.numpy as jnp
import ml_dtypes
import numpy as np
from jax import lax
from jax.experimental import pallas as pl
from jax.experimental.pallas import tpu as pltpu
from jax.sharding import PartitionSpec as P

MESH = pl.DeviceIdType.MESH
BF16 = jnp.bfloat16
F32 = jnp.float32
NLON = 1536
KMAX = 256
MEMBERS = 8
N_MEM = 4
N_LAT = 8
N_LON = 32
ROWS = 96
COLS = 48
LINES = 3
QUARTER = NLON // 4


def farthest_first(first, second, hops):
    steps = [(i, j) for i in range(first) for j in range(second) if i or j]
    return sorted(steps, key=lambda step: -hops(*step))


FAR_LON = farthest_first(8, 4, lambda i, j: min(i, 8 - i) + 2 * min(j, 4 - j))
FAR_ALL = sorted(
    [(k, *step) for k in range(4) for step in [(0, 0), *FAR_LON] if k or any(step)],
    key=lambda step: -(min(step[1], 8 - step[1]) + 2 * min(step[2], 4 - step[2]) + (step[0] > 0)),
)
FAR_GROUP = farthest_first(4, 8, lambda i, j: min(j, 8 - j) + (i > 0))


def halves(table):
    high = table.astype(ml_dtypes.bfloat16)
    low = (table - high.astype(np.float64)).astype(ml_dtypes.bfloat16)
    return np.stack([high, low])


def constants():
    piece, source, i = np.meshgrid(np.arange(3), np.arange(8), np.arange(16), indexing="ij")
    column = (48 * source + 16 * piece + i).reshape(-1)

    def table(columns, cosines, sines):
        angle = 2.0 * np.pi / NLON
        cos = np.cos((columns[:, None] * cosines[None] % NLON) * angle)
        sin = np.sin((columns[:, None] * sines[None] % NLON) * angle)
        return np.concatenate([cos, sin], axis=1) / 16.0

    c0, s0 = np.arange(0, 256, 4), np.arange(4, 257, 4)
    c2 = np.arange(2, 256, 4)
    c1 = np.arange(1, 256, 2)
    t0 = table(column, c0, s0)
    t2 = table(column, c2, c2)
    t1 = table(np.concatenate([column, QUARTER + column]), c1, c1)
    wave = np.concatenate([c0, s0, c2, c2, c1, c1])
    natural = np.concatenate([c0, 255 + s0, c2, 255 + c2, c1, 255 + c1])
    order = np.zeros((512, 512))
    order[np.arange(512), natural] = 1

    lines = np.zeros((288, 288))
    fields = np.zeros((2, 288, 2, 96))
    for quarter in range(4):
        for piece in range(3):
            for s in range(LINES):
                for m in range(MEMBERS):
                    row = (quarter * 3 + piece) * 24 + s * 8 + m
                    lines[row, ((m % 2) * 3 + piece) * 48 + (m // 2) * 12 + quarter * 3 + s] = 1
                    for f in range(2):
                        k, q = divmod(3 * f + piece, 2)
                        fields[f, row, :, q * 48 + k * 12 + quarter * 3 + s] = 1
    small = [a.astype(ml_dtypes.bfloat16) for a in (lines, fields.reshape(576, 192))]
    tables = [halves(t) for t in (t0, t2, t1, t0.T, t2.T, t1.T)]
    return small + tables + [order.astype(ml_dtypes.bfloat16), np.broadcast_to(wave, (8, 512)).astype(np.float32)]


def dot(a, b):
    return jnp.dot(a, b, preferred_element_type=F32)


def dot_nt(a, b):
    return lax.dot_general(a, b, (((1,), (1,)), ((), ())), preferred_element_type=F32)


def split(x):
    high = x.astype(BF16)
    return high, (x - high.astype(F32)).astype(BF16)


def dot3(x, table):
    high, low = split(x)
    both = dot(jnp.concatenate([high, low], axis=0), table[0])
    n = x.shape[0]
    return both[:n] + (both[n:] + dot(high, table[1]))


def kernel(p_ref, inn_in, wt_in, cell_in, lev_in, cut_in, *refs):
    n_const = 10
    loads_in = (inn_in, wt_in, cell_in, lev_in, p_ref, cut_in) + refs[:n_const]
    sets_ref, *factor_refs = refs[n_const : n_const + 3]
    scratch = refs[n_const + 3 :]
    n_load = n_const + 6
    loads_ref = scratch[:n_load]
    (packed, got, x_ref, g_ref, n_ref, c_ref, out_c, in_c, part1, sums1, part2, sums2, last, sets) = scratch[n_load : n_load + 14]
    load_sem, send_b, recv_b, send_c, recv_c, send_s, recv_s = scratch[n_load + 14 :]
    inn_ref, wt_ref, cell_ref, lev_ref, p_vmem, cut_ref, to_lines, to_fields, t0, t2, t1, b0, b2, b1, order, wave = loads_ref

    mem, lat, lon = lax.axis_index("mem"), lax.axis_index("lat"), lax.axis_index("lon")

    group = mem * N_LAT + lat
    depth, side = lon // 4, lax.rem(lon, 4)

    def lon_peer(d):
        return line_peer((0, *d))

    def group_peer(d):
        return {"mem": lax.rem(mem + d[0], N_MEM), "lat": lax.rem(lat + d[1], N_LAT), "lon": lon}

    def mem_peer(d):
        return {"mem": lax.rem(mem + d, N_MEM), "lat": lat, "lon": lon}

    def line_peer(d):
        return {
            "mem": lax.rem(mem + d[0], N_MEM),
            "lat": lat,
            "lon": lax.rem(depth + d[1], 8) * 4 + lax.rem(side + d[2], 4),
        }

    barrier = pltpu.get_barrier_semaphore()

    loads = [pltpu.make_async_copy(loads_in[k], loads_ref[k], load_sem.at[k]) for k in range(n_load)]
    for d in FAR_ALL[:64]:
        pl.semaphore_signal(barrier, inc=1, device_id=line_peer(d), device_id_type=MESH)
    for copy in loads[:5]:
        copy.start()
    for d in FAR_ALL[64:]:
        pl.semaphore_signal(barrier, inc=1, device_id=line_peer(d), device_id_type=MESH)
    for d in FAR_GROUP:
        if d[1]:
            pl.semaphore_signal(barrier, inc=1, device_id=group_peer(d), device_id_type=MESH)

    for copy in loads[5:]:
        copy.start()
    out_c[...] = jnp.zeros_like(out_c)

    for k in range(5):
        loads[k].wait()
    cell = cell_ref[...].astype(F32)
    row_of = jnp.floor((cell + 0.5) * (1.0 / COLS))
    col_of = cell - COLS * row_of
    key = row_of + ROWS * lev_ref[...].astype(F32)
    rows = lax.broadcasted_iota(jnp.int32, (4 * ROWS, 1), 0)
    row_hot = jnp.where(rows.astype(F32) == key, 1.0, 0.0).astype(BF16)
    lane_row = lax.broadcasted_iota(jnp.int32, (32, 1), 0)
    share = 2 * mem + jnp.where(lane_row >= 16, 1, 0)
    field = jnp.where(share >= 3, 1, 0) + jnp.where(share >= 6, 1, 0)
    column = (share - 3 * field) * 16 + lane_row - jnp.where(lane_row >= 16, 16, 0)
    hit = column.astype(F32) == col_of
    weight = wt_ref[...]
    scaled_d, scaled_w = split(weight * inn_ref[...]), split(weight)
    blank = jnp.zeros((ROWS, 2048), BF16)
    tile = jnp.zeros((4 * ROWS, 128), F32)
    for h in range(2):
        value = jnp.where(field == 0, scaled_d[h].astype(F32), jnp.where(field == 1, scaled_w[h].astype(F32), 0.0))
        placed = jnp.where(hit, value, 0.0).astype(BF16)
        tile += dot_nt(row_hot, jnp.concatenate([blank, placed], axis=0))
    same = lax.broadcasted_iota(jnp.int32, (ROWS, ROWS), 0) == lax.broadcasted_iota(jnp.int32, (ROWS, ROWS), 1)
    eye = jnp.where(same, 1.0, 0.0).astype(BF16)
    for k in range(N_MEM):
        both = jnp.concatenate([p_vmem[0, k], p_vmem[1, k], jnp.zeros((32, ROWS), BF16)], axis=0)
        message = dot_nt(eye, both) + tile[k * ROWS : (k + 1) * ROWS]
        packed[k] = message.reshape(N_LON, LINES, 1, 128)

    pl.semaphore_wait(barrier, 155)

    place_here = (lax.rem(lon, 8) * 4 + mem) * 4 + lon // 8
    for d in FAR_ALL:
        peer = line_peer(d)
        pltpu.make_async_remote_copy(
            packed.at[peer["mem"], peer["lon"]], got.at[place_here], send_b, recv_b, device_id=peer, device_id_type=MESH
        ).start()

    got[place_here] = packed[mem, lon]
    for copy in loads[5:]:
        copy.wait()
    this_level = lax.broadcasted_iota(jnp.int32, (1, N_MEM), 1) == mem
    cutoff = jnp.sum(jnp.where(this_level, cut_ref[...].astype(F32), 0.0), keepdims=True)
    scaled = wave[0:1, :] / cutoff
    spectrum = 1.0 / (1.0 + scaled * scaled)
    lots = got.at[pl.ds(0, 127)]
    pltpu.make_async_copy(lots, lots, recv_b).wait()

    lane = lax.broadcasted_iota(jnp.int32, (48, 128), 1)
    blocks = [got[16 * k : 16 * k + 16].reshape(48, 128) for k in range(8)]
    for bit in range(3):
        width = 16 << bit
        low_side = (lane & width) == 0
        for k in range(8):
            if not k & (1 << bit):
                a, b = blocks[k], blocks[k | (1 << bit)]
                blocks[k] = jnp.where(low_side, a, pltpu.roll(b, width, 1))
                blocks[k | (1 << bit)] = jnp.where(low_side, pltpu.roll(a, 128 - width, 1), b)
    x_all = dot(to_lines[...], jnp.concatenate(blocks[:6], axis=0).astype(BF16))
    f_all = dot(to_fields[...], jnp.concatenate(split(jnp.concatenate(blocks[6:], axis=0)), axis=0))
    for t in range(12):
        x_ref[:, t * 128 : t * 128 + 128] = x_all[t * 24 : t * 24 + 24]
        g_ref[:, t * 128 : t * 128 + 128] = f_all[t * 24 : t * 24 + 24]
        n_ref[:, t * 128 : t * 128 + 128] = f_all[288 + t * 24 : 288 + t * 24 + 24]

    def quarters(x):
        return [x[:, k * QUARTER : (k + 1) * QUARTER] for k in range(4)]

    def analyse(field):
        q0, q1, q2, q3 = quarters(x_ref[...] * field)
        even, odd = q0 + q2, q1 + q3
        found = [
            dot3(even + odd, t0),
            dot3(even - odd, t2),
            dot3(jnp.concatenate([q0 - q2, q1 - q3], axis=1), t1),
        ]
        return jnp.concatenate(found, axis=1) * spectrum

    def synthesize(coeffs):
        scaled = coeffs * spectrum
        e0 = dot3(scaled[:, :128], b0)
        e2 = dot3(scaled[:, 128:256], b2)
        o = dot3(scaled[:, 256:], b1)
        oa, ob = o[:, :QUARTER], o[:, QUARTER:]
        plus, minus = e0 + e2, e0 - e2
        line = jnp.concatenate([plus + oa, minus + ob, plus - oa, minus - ob], axis=1)
        seen = (x_ref[...] * line).reshape(LINES, MEMBERS, NLON)
        total = jnp.sum(seen, axis=1, keepdims=True)
        return jnp.broadcast_to(total, (LINES, MEMBERS, NLON)).reshape(LINES * MEMBERS, NLON)

    def send_coeffs(v, coeffs):
        c_ref[...] = coeffs
        for k in range(N_MEM):
            for m in range(2):
                for s in range(LINES):
                    out_c[v, k, m * LINES + s : m * LINES + s + 1, :] = c_ref[s * 8 + 2 * k + m : s * 8 + 2 * k + m + 1, :]
        for d in (2, 3, 1):
            peer = mem_peer(d)
            pltpu.make_async_remote_copy(
                out_c.at[v, peer["mem"]], in_c.at[v, mem], send_c.at[v], recv_c.at[v], device_id=peer, device_id_type=MESH
            ).start()
        in_c[v, mem] = out_c[v, mem]

    def total_of(x):
        return jnp.sum(x, keepdims=True)

    f0 = g_ref[...]
    coeffs = analyse(f0)
    send_coeffs(0, coeffs)
    u0 = synthesize(coeffs)
    f1 = n_ref[...] * u0
    m1, m2 = total_of(f0 * u0), total_of(f1 * u0)
    coeffs = analyse(f1)
    send_coeffs(1, coeffs)
    u1 = synthesize(coeffs)
    f2 = n_ref[...] * u1
    m3, m4 = total_of(f1 * u1), total_of(f2 * u1)

    place = lax.broadcasted_iota(jnp.int32, (1, 128), 1)
    own = jnp.zeros((1, 128), F32)
    for k, value in enumerate((m1, m2, m3, m4)):
        own = jnp.where(place == k, value, own)

    def send_sums(stage, part, sums, peer_of, index):
        for d in (FAR_GROUP, FAR_LON)[stage]:
            pltpu.make_async_remote_copy(
                part, sums.at[index], send_s.at[stage], recv_s.at[stage], device_id=peer_of(d), device_id_type=MESH
            ).start()

    def wait_sums(stage, sums):
        lots = sums.at[pl.ds(0, sums.shape[0] - 1)]
        pltpu.make_async_copy(lots, lots, recv_s.at[stage]).wait()
        return jnp.sum(sums[...], axis=0)

    part1[...] = own
    send_sums(0, part1, sums1, group_peer, group)
    sums1[group] = own
    send_coeffs(2, analyse(f2))
    own = wait_sums(0, sums1)
    part2[...] = own
    send_sums(1, part2, sums2, lon_peer, lon)
    sums2[lon] = own
    three = in_c.at[0, pl.ds(0, 3)]
    for v in range(3):
        pltpu.make_async_copy(three, three, recv_c.at[v]).wait()
    for v in range(3):
        both = dot(jnp.concatenate(split(in_c[v].reshape(32, 512)), axis=0), order[...])
        last[...] = (both[:32] + both[32:]).reshape(N_MEM, 8, 512)
        for m in range(2):
            for s in range(LINES):
                for k in range(N_MEM):
                    sets[v, m, s, k : k + 1, :] = last[k, m * LINES + s : m * LINES + s + 1, :]
    sets_out = pltpu.make_async_copy(sets, sets_ref, load_sem.at[n_load])
    sets_out.start()
    moments = wait_sums(1, sums2)
    m1, m2, m3, m4 = (total_of(jnp.where(place == k, moments, 0.0)) for k in range(4))

    step = m1 / (m1 + m2)
    rest = 1.0 - step
    norm = rest * rest * m1 - 2.0 * step * rest * m2 + step * step * m3
    growth = norm / m1
    a = rest + growth
    curved = a * a * (m1 + m2) - 2.0 * a * step * (m2 + m3) + step * step * (m3 + m4)
    step_next = norm / curved
    factors = (
        step + step_next * a,
        -step_next * step,
        rest - step_next * a,
        -step - step_next * (a - step),
        step_next * step,
    )
    for k, factor in enumerate((*factors[:2], jnp.zeros((1, 1), F32), *factors[2:])):
        factor_refs[k // 3][k % 3 : k % 3 + 1, :] = jnp.broadcast_to(factor, (1, 512))
    sets_out.wait()

    lots = got.at[pl.ds(0, 127)]
    pltpu.make_async_copy(lots, lots, send_b).wait()
    three = in_c.at[0, pl.ds(0, 3)]
    for v in range(3):
        pltpu.make_async_copy(three, three, send_c.at[v]).wait()
    for stage, sums in enumerate((sums1, sums2)):
        lots = sums.at[pl.ds(0, sums.shape[0] - 1)]
        pltpu.make_async_copy(lots, lots, send_s.at[stage]).wait()


def body(perturbations, innovation, obs_weight, obs_cell, obs_level, cutoff):
    consts = [jnp.asarray(c) for c in constants()]
    vmem = pl.BlockSpec(memory_space=pltpu.VMEM)
    anywhere = pl.BlockSpec(memory_space=pl.ANY)
    sets_shape = jax.ShapeDtypeStruct((3, 2, LINES, N_MEM, 2 * KMAX), F32)
    factor_shape = jax.ShapeDtypeStruct((3, 2 * KMAX), F32)
    dma = pltpu.SemaphoreType.DMA
    obs = (innovation, obs_weight, obs_cell, obs_level)
    turned = jnp.swapaxes(perturbations, 2, 3)
    limits = cutoff.reshape(1, N_MEM)
    scratch = [pltpu.VMEM(c.shape, c.dtype) for c in (*obs, turned, limits, *consts)] + [
        pltpu.VMEM((N_MEM, N_LON, LINES, 1, 128), F32),
        pltpu.VMEM((N_MEM * N_LON, LINES, 1, 128), F32),
        pltpu.VMEM((24, NLON), F32),
        pltpu.VMEM((24, NLON), F32),
        pltpu.VMEM((24, NLON), F32),
        pltpu.VMEM((24, 512), F32),
        pltpu.VMEM((3, 4, 8, 512), F32),
        pltpu.VMEM((3, 4, 8, 512), F32),
        pltpu.VMEM((1, 128), F32),
        pltpu.VMEM((N_LON, 1, 128), F32),
        pltpu.VMEM((1, 128), F32),
        pltpu.VMEM((N_MEM * N_LAT, 1, 128), F32),
        pltpu.VMEM((N_MEM, 8, 512), F32),
        pltpu.VMEM((3, 2, LINES, N_MEM, 512), F32),
        dma((len(obs) + 2 + len(consts) + 1,)),
        dma,
        dma,
        dma((3,)),
        dma((3,)),
        dma((2,)),
        dma((2,)),
    ]
    sets, *f = pl.pallas_call(
        kernel,
        out_shape=(sets_shape,) + (factor_shape,) * 2,
        in_specs=[anywhere] * (6 + len(consts)),
        out_specs=(anywhere,) + (vmem,) * 2,
        scratch_shapes=scratch,
        compiler_params=pltpu.CompilerParams(
            collective_id=0, has_side_effects=True, vmem_limit_bytes=60 * 1024 * 1024
        ),
    )(turned, *obs, limits, *consts)
    found, left = (jnp.sum(factor[:, None, None, None] * sets, axis=0) for factor in f)
    return jnp.swapaxes(found, 1, 2), jnp.swapaxes(left, 1, 2)


def solution(mesh):
    in_specs = (
        P("mem", None, "lat", "lon"),
        P("lat", "lon"),
        P("lat", "lon"),
        P("lat", "lon"),
        P("lat", "lon"),
        P(),
    )
    out_specs = (P("mem", None, ("lat", "lon"), None), P("mem", None, ("lat", "lon"), None))
    return jax.shard_map(body, mesh=mesh, in_specs=in_specs, out_specs=out_specs, check_vma=False)
```

```python
import jax
import jax.numpy as jnp
import ml_dtypes
import numpy as np
from jax import lax
from jax.experimental import pallas as pl
from jax.experimental.pallas import tpu as pltpu
from jax.sharding import PartitionSpec as P

MESH = pl.DeviceIdType.MESH
BF16 = jnp.bfloat16
F32 = jnp.float32
NLON = 1536
KMAX = 256
MEMBERS = 8
N_MEM = 4
N_LAT = 8
N_LON = 32
ROWS = 96
COLS = 48
LINES = 3
QUARTER = NLON // 4


def farthest_first(first, second, hops):
    steps = [(i, j) for i in range(first) for j in range(second) if i or j]
    return sorted(steps, key=lambda step: -hops(*step))


FAR_LON = farthest_first(8, 4, lambda i, j: min(i, 8 - i) + 2 * min(j, 4 - j))
FAR_ALL = sorted(
    [(k, *step) for k in range(4) for step in [(0, 0), *FAR_LON] if k or any(step)],
    key=lambda step: -(min(step[1], 8 - step[1]) + 2 * min(step[2], 4 - step[2]) + (step[0] > 0)),
)
FAR_GROUP = farthest_first(4, 8, lambda i, j: min(j, 8 - j) + (i > 0))


def halves(table):
    high = table.astype(ml_dtypes.bfloat16)
    low = (table - high.astype(np.float64)).astype(ml_dtypes.bfloat16)
    return np.stack([high, low])


def constants():
    piece, source, i = np.meshgrid(np.arange(3), np.arange(8), np.arange(16), indexing="ij")
    column = (48 * source + 16 * piece + i).reshape(-1)

    def table(columns, cosines, sines):
        angle = 2.0 * np.pi / NLON
        cos = np.cos((columns[:, None] * cosines[None] % NLON) * angle)
        sin = np.sin((columns[:, None] * sines[None] % NLON) * angle)
        return np.concatenate([cos, sin], axis=1) / 16.0

    c0, s0 = np.arange(0, 256, 4), np.arange(4, 257, 4)
    c2 = np.arange(2, 256, 4)
    c1 = np.arange(1, 256, 2)
    t0 = table(column, c0, s0)
    t2 = table(column, c2, c2)
    t1 = table(np.concatenate([column, QUARTER + column]), c1, c1)
    wave = np.concatenate([c0, s0, c2, c2, c1, c1])
    natural = np.concatenate([c0, 255 + s0, c2, 255 + c2, c1, 255 + c1])
    order = np.zeros((512, 512))
    order[np.arange(512), natural] = 1

    lines = np.zeros((288, 288))
    fields = np.zeros((2, 288, 2, 96))
    for quarter in range(4):
        for piece in range(3):
            for s in range(LINES):
                for m in range(MEMBERS):
                    row = (quarter * 3 + piece) * 24 + s * 8 + m
                    lines[row, ((m % 2) * 3 + piece) * 48 + (m // 2) * 12 + quarter * 3 + s] = 1
                    for f in range(2):
                        k, q = divmod(3 * f + piece, 2)
                        fields[f, row, :, q * 48 + k * 12 + quarter * 3 + s] = 1
    small = [a.astype(ml_dtypes.bfloat16) for a in (lines, fields.reshape(576, 192))]
    tables = [halves(t) for t in (t0, t2, t1, t0.T, t2.T, t1.T)]
    return small + tables + [order.astype(ml_dtypes.bfloat16), np.broadcast_to(wave, (8, 512)).astype(np.float32)]


def dot(a, b):
    return jnp.dot(a, b, preferred_element_type=F32)


def dot_nt(a, b):
    return lax.dot_general(a, b, (((1,), (1,)), ((), ())), preferred_element_type=F32)


def split(x):
    high = x.astype(BF16)
    return high, (x - high.astype(F32)).astype(BF16)


def dot3(x, table):
    high, low = split(x)
    both = dot(jnp.concatenate([high, low], axis=0), table[0])
    n = x.shape[0]
    return both[:n] + (both[n:] + dot(high, table[1]))


def kernel(p_ref, inn_in, wt_in, cell_in, lev_in, cut_in, *refs):
    n_const = 10
    loads_in = (inn_in, wt_in, cell_in, lev_in, p_ref, cut_in) + refs[:n_const]
    sets_ref, *factor_refs = refs[n_const : n_const + 3]
    scratch = refs[n_const + 3 :]
    n_load = n_const + 6
    loads_ref = scratch[:n_load]
    (packed, got, x_ref, g_ref, n_ref, c_ref, out_c, in_c, part1, sums1, part2, sums2, last, sets) = scratch[n_load : n_load + 14]
    load_sem, send_b, recv_b, send_c, recv_c, send_s, recv_s = scratch[n_load + 14 :]
    inn_ref, wt_ref, cell_ref, lev_ref, p_vmem, cut_ref, to_lines, to_fields, t0, t2, t1, b0, b2, b1, order, wave = loads_ref

    mem, lat, lon = lax.axis_index("mem"), lax.axis_index("lat"), lax.axis_index("lon")

    group = mem * N_LAT + lat
    depth, side = lon // 4, lax.rem(lon, 4)

    def lon_peer(d):
        return line_peer((0, *d))

    def group_peer(d):
        return {"mem": lax.rem(mem + d[0], N_MEM), "lat": lax.rem(lat + d[1], N_LAT), "lon": lon}

    def mem_peer(d):
        return {"mem": lax.rem(mem + d, N_MEM), "lat": lat, "lon": lon}

    def line_peer(d):
        return {
            "mem": lax.rem(mem + d[0], N_MEM),
            "lat": lat,
            "lon": lax.rem(depth + d[1], 8) * 4 + lax.rem(side + d[2], 4),
        }

    barrier = pltpu.get_barrier_semaphore()

    loads = [pltpu.make_async_copy(loads_in[k], loads_ref[k], load_sem.at[k]) for k in range(n_load)]
    for d in FAR_ALL[:64]:
        pl.semaphore_signal(barrier, inc=1, device_id=line_peer(d), device_id_type=MESH)
    for copy in loads[:5]:
        copy.start()
    for d in FAR_ALL[64:]:
        pl.semaphore_signal(barrier, inc=1, device_id=line_peer(d), device_id_type=MESH)
    for d in FAR_GROUP:
        if d[1]:
            pl.semaphore_signal(barrier, inc=1, device_id=group_peer(d), device_id_type=MESH)

    for copy in loads[5:]:
        copy.start()
    out_c[...] = jnp.zeros_like(out_c)

    for k in range(5):
        loads[k].wait()
    cell = cell_ref[...].astype(F32)
    row_of = jnp.floor((cell + 0.5) * (1.0 / COLS))
    col_of = cell - COLS * row_of
    key = row_of + ROWS * lev_ref[...].astype(F32)
    rows = lax.broadcasted_iota(jnp.int32, (4 * ROWS, 1), 0)
    row_hot = jnp.where(rows.astype(F32) == key, 1.0, 0.0).astype(BF16)
    lane_row = lax.broadcasted_iota(jnp.int32, (32, 1), 0)
    share = 2 * mem + jnp.where(lane_row >= 16, 1, 0)
    field = jnp.where(share >= 3, 1, 0) + jnp.where(share >= 6, 1, 0)
    column = (share - 3 * field) * 16 + lane_row - jnp.where(lane_row >= 16, 16, 0)
    hit = column.astype(F32) == col_of
    weight = wt_ref[...]
    scaled_d, scaled_w = split(weight * inn_ref[...]), split(weight)
    blank = jnp.zeros((ROWS, 2048), BF16)
    tile = jnp.zeros((4 * ROWS, 128), F32)
    for h in range(2):
        value = jnp.where(field == 0, scaled_d[h].astype(F32), jnp.where(field == 1, scaled_w[h].astype(F32), 0.0))
        placed = jnp.where(hit, value, 0.0).astype(BF16)
        tile += dot_nt(row_hot, jnp.concatenate([blank, placed], axis=0))
    same = lax.broadcasted_iota(jnp.int32, (ROWS, ROWS), 0) == lax.broadcasted_iota(jnp.int32, (ROWS, ROWS), 1)
    eye = jnp.where(same, 1.0, 0.0).astype(BF16)
    for k in range(N_MEM):
        both = jnp.concatenate([p_vmem[0, k], p_vmem[1, k], jnp.zeros((32, ROWS), BF16)], axis=0)
        message = dot_nt(eye, both) + tile[k * ROWS : (k + 1) * ROWS]
        packed[k] = message.reshape(N_LON, LINES, 1, 128)

    pl.semaphore_wait(barrier, 155)

    place_here = (lax.rem(lon, 8) * 4 + mem) * 4 + lon // 8
    for d in FAR_ALL:
        peer = line_peer(d)
        pltpu.make_async_remote_copy(
            packed.at[peer["mem"], peer["lon"]], got.at[place_here], send_b, recv_b, device_id=peer, device_id_type=MESH
        ).start()

    got[place_here] = packed[mem, lon]
    for copy in loads[5:]:
        copy.wait()
    this_level = lax.broadcasted_iota(jnp.int32, (1, N_MEM), 1) == mem
    cutoff = jnp.sum(jnp.where(this_level, cut_ref[...].astype(F32), 0.0), keepdims=True)
    scaled = wave[0:1, :] / cutoff
    spectrum = 1.0 / (1.0 + scaled * scaled)
    lots = got.at[pl.ds(0, 127)]
    pltpu.make_async_copy(lots, lots, recv_b).wait()

    lane = lax.broadcasted_iota(jnp.int32, (48, 128), 1)
    blocks = [got[16 * k : 16 * k + 16].reshape(48, 128) for k in range(8)]
    for bit in range(3):
        width = 16 << bit
        low_side = (lane & width) == 0
        for k in range(8):
            if not k & (1 << bit):
                a, b = blocks[k], blocks[k | (1 << bit)]
                blocks[k] = jnp.where(low_side, a, pltpu.roll(b, width, 1))
                blocks[k | (1 << bit)] = jnp.where(low_side, pltpu.roll(a, 128 - width, 1), b)
    x_all = dot(to_lines[...], jnp.concatenate(blocks[:6], axis=0).astype(BF16))
    f_all = dot(to_fields[...], jnp.concatenate(split(jnp.concatenate(blocks[6:], axis=0)), axis=0))
    for t in range(12):
        x_ref[:, t * 128 : t * 128 + 128] = x_all[t * 24 : t * 24 + 24]
        g_ref[:, t * 128 : t * 128 + 128] = f_all[t * 24 : t * 24 + 24]
        n_ref[:, t * 128 : t * 128 + 128] = f_all[288 + t * 24 : 288 + t * 24 + 24]

    def quarters(x):
        return [x[:, k * QUARTER : (k + 1) * QUARTER] for k in range(4)]

    def analyse(field):
        q0, q1, q2, q3 = quarters(x_ref[...] * field)
        even, odd = q0 + q2, q1 + q3
        found = [
            dot3(even + odd, t0),
            dot3(even - odd, t2),
            dot3(jnp.concatenate([q0 - q2, q1 - q3], axis=1), t1),
        ]
        return jnp.concatenate(found, axis=1) * spectrum

    def synthesize(coeffs):
        scaled = coeffs * spectrum
        e0 = dot3(scaled[:, :128], b0)
        e2 = dot3(scaled[:, 128:256], b2)
        o = dot3(scaled[:, 256:], b1)
        oa, ob = o[:, :QUARTER], o[:, QUARTER:]
        plus, minus = e0 + e2, e0 - e2
        line = jnp.concatenate([plus + oa, minus + ob, plus - oa, minus - ob], axis=1)
        seen = (x_ref[...] * line).reshape(LINES, MEMBERS, NLON)
        total = jnp.sum(seen, axis=1, keepdims=True)
        return jnp.broadcast_to(total, (LINES, MEMBERS, NLON)).reshape(LINES * MEMBERS, NLON)

    def send_coeffs(v, coeffs):
        c_ref[...] = coeffs
        for k in range(N_MEM):
            for m in range(2):
                for s in range(LINES):
                    out_c[v, k, m * LINES + s : m * LINES + s + 1, :] = c_ref[s * 8 + 2 * k + m : s * 8 + 2 * k + m + 1, :]
        for d in (2, 3, 1):
            peer = mem_peer(d)
            pltpu.make_async_remote_copy(
                out_c.at[v, peer["mem"]], in_c.at[v, mem], send_c.at[v], recv_c.at[v], device_id=peer, device_id_type=MESH
            ).start()
        in_c[v, mem] = out_c[v, mem]

    def total_of(x):
        return jnp.sum(x, keepdims=True)

    f0 = g_ref[...]
    coeffs0 = analyse(f0)
    u0 = synthesize(coeffs0)
    f1 = n_ref[...] * u0
    m1, m2 = total_of(f0 * u0), total_of(f1 * u0)
    coeffs1 = analyse(f1)
    u1 = synthesize(coeffs1)
    f2 = n_ref[...] * u1
    m3, m4 = total_of(f1 * u1), total_of(f2 * u1)

    place = lax.broadcasted_iota(jnp.int32, (1, 128), 1)
    own = jnp.zeros((1, 128), F32)
    for k, value in enumerate((m1, m2, m3, m4)):
        own = jnp.where(place == k, value, own)

    def send_sums(stage, part, sums, peer_of, index):
        for d in (FAR_GROUP, FAR_LON)[stage]:
            pltpu.make_async_remote_copy(
                part, sums.at[index], send_s.at[stage], recv_s.at[stage], device_id=peer_of(d), device_id_type=MESH
            ).start()

    def wait_sums(stage, sums):
        lots = sums.at[pl.ds(0, sums.shape[0] - 1)]
        pltpu.make_async_copy(lots, lots, recv_s.at[stage]).wait()
        return jnp.sum(sums[...], axis=0)

    part1[...] = own
    send_sums(0, part1, sums1, group_peer, group)
    sums1[group] = own
    send_coeffs(0, coeffs0)
    send_coeffs(1, coeffs1)
    send_coeffs(2, analyse(f2))
    own = wait_sums(0, sums1)
    part2[...] = own
    send_sums(1, part2, sums2, lon_peer, lon)
    sums2[lon] = own
    three = in_c.at[0, pl.ds(0, 3)]
    for v in range(3):
        pltpu.make_async_copy(three, three, recv_c.at[v]).wait()
    for v in range(3):
        both = dot(jnp.concatenate(split(in_c[v].reshape(32, 512)), axis=0), order[...])
        last[...] = (both[:32] + both[32:]).reshape(N_MEM, 8, 512)
        for m in range(2):
            for s in range(LINES):
                for k in range(N_MEM):
                    sets[v, m, s, k : k + 1, :] = last[k, m * LINES + s : m * LINES + s + 1, :]
    sets_out = pltpu.make_async_copy(sets, sets_ref, load_sem.at[n_load])
    sets_out.start()
    moments = wait_sums(1, sums2)
    m1, m2, m3, m4 = (total_of(jnp.where(place == k, moments, 0.0)) for k in range(4))

    step = m1 / (m1 + m2)
    rest = 1.0 - step
    norm = rest * rest * m1 - 2.0 * step * rest * m2 + step * step * m3
    growth = norm / m1
    a = rest + growth
    curved = a * a * (m1 + m2) - 2.0 * a * step * (m2 + m3) + step * step * (m3 + m4)
    step_next = norm / curved
    factors = (
        step + step_next * a,
        -step_next * step,
        rest - step_next * a,
        -step - step_next * (a - step),
        step_next * step,
    )
    for k, factor in enumerate((*factors[:2], jnp.zeros((1, 1), F32), *factors[2:])):
        factor_refs[k // 3][k % 3 : k % 3 + 1, :] = jnp.broadcast_to(factor, (1, 512))
    sets_out.wait()

    lots = got.at[pl.ds(0, 127)]
    pltpu.make_async_copy(lots, lots, send_b).wait()
    three = in_c.at[0, pl.ds(0, 3)]
    for v in range(3):
        pltpu.make_async_copy(three, three, send_c.at[v]).wait()
    for stage, sums in enumerate((sums1, sums2)):
        lots = sums.at[pl.ds(0, sums.shape[0] - 1)]
        pltpu.make_async_copy(lots, lots, send_s.at[stage]).wait()


def body(perturbations, innovation, obs_weight, obs_cell, obs_level, cutoff):
    consts = [jnp.asarray(c) for c in constants()]
    vmem = pl.BlockSpec(memory_space=pltpu.VMEM)
    anywhere = pl.BlockSpec(memory_space=pl.ANY)
    sets_shape = jax.ShapeDtypeStruct((3, 2, LINES, N_MEM, 2 * KMAX), F32)
    factor_shape = jax.ShapeDtypeStruct((3, 2 * KMAX), F32)
    dma = pltpu.SemaphoreType.DMA
    obs = (innovation, obs_weight, obs_cell, obs_level)
    turned = jnp.swapaxes(perturbations, 2, 3)
    limits = cutoff.reshape(1, N_MEM)
    scratch = [pltpu.VMEM(c.shape, c.dtype) for c in (*obs, turned, limits, *consts)] + [
        pltpu.VMEM((N_MEM, N_LON, LINES, 1, 128), F32),
        pltpu.VMEM((N_MEM * N_LON, LINES, 1, 128), F32),
        pltpu.VMEM((24, NLON), F32),
        pltpu.VMEM((24, NLON), F32),
        pltpu.VMEM((24, NLON), F32),
        pltpu.VMEM((24, 512), F32),
        pltpu.VMEM((3, 4, 8, 512), F32),
        pltpu.VMEM((3, 4, 8, 512), F32),
        pltpu.VMEM((1, 128), F32),
        pltpu.VMEM((N_LON, 1, 128), F32),
        pltpu.VMEM((1, 128), F32),
        pltpu.VMEM((N_MEM * N_LAT, 1, 128), F32),
        pltpu.VMEM((N_MEM, 8, 512), F32),
        pltpu.VMEM((3, 2, LINES, N_MEM, 512), F32),
        dma((len(obs) + 2 + len(consts) + 1,)),
        dma,
        dma,
        dma((3,)),
        dma((3,)),
        dma((2,)),
        dma((2,)),
    ]
    sets, *f = pl.pallas_call(
        kernel,
        out_shape=(sets_shape,) + (factor_shape,) * 2,
        in_specs=[anywhere] * (6 + len(consts)),
        out_specs=(anywhere,) + (vmem,) * 2,
        scratch_shapes=scratch,
        compiler_params=pltpu.CompilerParams(
            collective_id=0, has_side_effects=True, vmem_limit_bytes=60 * 1024 * 1024
        ),
    )(turned, *obs, limits, *consts)
    found, left = (jnp.sum(factor[:, None, None, None] * sets, axis=0) for factor in f)
    return jnp.swapaxes(found, 1, 2), jnp.swapaxes(left, 1, 2)


def solution(mesh):
    in_specs = (
        P("mem", None, "lat", "lon"),
        P("lat", "lon"),
        P("lat", "lon"),
        P("lat", "lon"),
        P("lat", "lon"),
        P(),
    )
    out_specs = (P("mem", None, ("lat", "lon"), None), P("mem", None, ("lat", "lon"), None))
    return jax.shard_map(body, mesh=mesh, in_specs=in_specs, out_specs=out_specs, check_vma=False)
```
